32 devices in a mesh: feat: 8 (over y, x, core), rep: 4 (over z).
Axes of the slice: x: 2, y: 2, z: 4, core: 2. Of those that a mesh axis runs over, the one named last changes fastest.
Arguments:
- feats: bfloat16 [4, 2048, 1024], P('rep', None, 'feat'), may hold values from -6 to 6
- w_self: bfloat16 [1024, 256], P('feat'), may hold values from -0.1875 to 0.1875
- w_neigh: bfloat16 [1024, 256], P('feat'), may hold values from -0.1875 to 0.1875
- bias: float32 [256], replicated, may hold values from -3 to 3
- tile_weight: bfloat16 [4, 8, 3, 128, 128], P('rep'), may hold values from -0.375 to 0.375
- tile_src: int32 [4, 8, 3], P('rep'), may hold values from 0 to 15
- tile_count: int32 [4, 8], P('rep'), may hold values from 1 to 3
- owner_order: int32 [4, 8], P('rep'), may hold values from 0 to 7, each once within a row
- cotangent: bfloat16 [4, 1024, 256], P('rep', 'feat'), may hold values from -6 to 6
Outputs:
- hidden: bfloat16 [4, 1024, 256], P('rep', 'feat')
- grad_self: float32 [1024, 256], P('feat')
- grad_neigh: float32 [1024, 256], P('feat')
The draws below stay inside these ranges and needn't reach their ends.
All inputs are finite; a program needn't handle non-finite values.
Results may differ from the reference program's by a relative error of at most 0.0055.
Values may be sent and summed in bfloat16 or wider, within the bound.
No kernel may reach another device: no remote copies, remote signals or barrier semaphores. Data moves between devices by JAX's collectives and lax.ppermute only.
A program may use at most 64 MiB of HBM per device.

```python
import jax
import jax.numpy as jnp
from jax import lax

F = 1024
H = 256
BLOCK = 128
KMAX = 3
NDB = 8
NSB = 16
N_REP = 4


def set_ends(entries, own_key, low, largest):
    shape = entries.shape
    index_at = [jax.random.randint(jax.random.fold_in(own_key, axis), (), 0, shape[axis]) for axis in range(len(shape))]
    entries = entries.at[tuple(index_at)].set(low)
    longest = shape.index(max(shape))
    index_at[longest] = (index_at[longest] + 1) % shape[longest]
    return entries.at[tuple(index_at)].set(largest)


def strengthened(values, rng, source, target, shards_of, factor):
    owner, partner = [(jnp.arange(values.shape[dim]) // (values.shape[dim] // shards_of)).reshape([-1 if axis == dim else 1 for axis in range(values.ndim)]) for dim in (source, target)]
    chosen = jax.random.permutation(rng, shards_of)[partner]
    strong = (owner == chosen) | (owner == (partner + shards_of // 2) % shards_of)
    return jnp.where(strong, factor * values, values)


def shard_levels(stream_key, dims, pieces, low, high):
    loudness, own = 1.0, jax.random.fold_in(stream_key, 6)
    for axis_at, blocks in pieces:
        draws = jnp.exp(jax.random.uniform(jax.random.fold_in(own, axis_at), (blocks,), jnp.float32, low / len(pieces), high / len(pieces)))
        loudness = loudness * jnp.repeat(draws, dims[axis_at] // blocks).reshape([-1 if axis == axis_at else 1 for axis in range(len(dims))])
    return loudness


def centred(own_key, dims, scale, bound, cuts=(), held_as=jnp.bfloat16):
    result = scale * jax.random.normal(own_key, dims, jnp.float32)
    if cuts:
        result = result * shard_levels(own_key, dims, cuts, -0.22, 0.18)
    return jnp.clip(result, -bound, bound).astype(held_as)


def noise_with(rng, extent, scale, reach, pieces, heavy, held_as=jnp.bfloat16):
    entries = scale * jax.random.normal(rng, extent, jnp.float32)
    if pieces:
        entries = entries * shard_levels(rng, extent, pieces, -0.22, 0.18)
    return jnp.clip(strengthened(entries, jax.random.fold_in(rng, 3), *heavy), -reach, reach).astype(held_as)


def setup_inputs(seed: int = 0) -> dict:
    seeds = jax.random.split(jax.random.key(seed), 10)
    feats = noise_with(seeds[0], (N_REP, NSB * BLOCK, F), 1.0, 6.0, ((0, 4), (2, 8)), (2, 1, 8, 2.0))
    w_self = centred(seeds[1], (F, H), F ** -0.5, 0.1875, ((0, 8),))
    w_neigh = centred(seeds[2], (F, H), F ** -0.5, 0.1875, ((0, 8),))
    bias = centred(seeds[3], (H,), 0.5, 3.0, (), jnp.float32)
    tile_weight = centred(seeds[4], (N_REP, NDB, KMAX, BLOCK, BLOCK), 0.0625, 0.375, ((0, 4),))
    tile_src = set_ends(jax.random.randint(seeds[5], (N_REP, NDB, KMAX), 0, NSB), jax.random.fold_in(seeds[5], 1), 0, NSB - 1).astype(jnp.int32)
    tile_count = set_ends(jax.random.randint(seeds[6], (N_REP, NDB), 1, KMAX + 1), jax.random.fold_in(seeds[6], 1), 1, KMAX).astype(jnp.int32)
    owner_order = jax.vmap(lambda own: jax.random.permutation(own, NDB))(jax.random.split(seeds[7], N_REP)).reshape((N_REP, NDB)).astype(jnp.int32)
    cotangent = centred(seeds[8], (N_REP, NDB * BLOCK, H), 1.0, 6.0, ((0, 4), (1, 8)))
    return {"feats": feats, "w_self": w_self, "w_neigh": w_neigh, "bias": bias, "tile_weight": tile_weight, "tile_src": tile_src, "tile_count": tile_count, "owner_order": owner_order, "cotangent": cotangent}


def one_batch(inputs):
    feats, tile_weight, tile_src, tile_count, owner_order, cotangent, w_self, w_neigh, bias = inputs
    by_block = feats.reshape(NSB, BLOCK, F)
    in_use = jnp.arange(KMAX)[None, :] < tile_count[:, None]
    masked = jnp.where(in_use[:, :, None, None], tile_weight, jnp.zeros((), jnp.bfloat16))
    sources = by_block[tile_src]
    aggregate = jnp.einsum("bkij,bkjc->bic", masked.astype(jnp.float32), sources.astype(jnp.float32)).astype(jnp.bfloat16)
    target_rows = by_block[owner_order].reshape(-1, F)
    target_mean = aggregate[owner_order].reshape(-1, F)
    preact = jnp.dot(target_rows, w_self, preferred_element_type=jnp.float32)
    preact = preact + jnp.dot(target_mean, w_neigh, preferred_element_type=jnp.float32) + bias
    hidden = jax.nn.silu(preact).astype(jnp.bfloat16)
    squash = jax.nn.sigmoid(preact)
    output_grad = (cotangent.astype(jnp.float32) * squash * (1.0 + preact * (1.0 - squash))).astype(jnp.bfloat16)
    grad_self = jnp.dot(target_rows.T, output_grad, preferred_element_type=jnp.float32)
    grad_neigh = jnp.dot(target_mean.T, output_grad, preferred_element_type=jnp.float32)
    return hidden, grad_self, grad_neigh


def reference(feats, w_self, w_neigh, bias, tile_weight, tile_src, tile_count, owner_order, cotangent):
    def wrapped(inputs):
        return one_batch(inputs + (w_self, w_neigh, bias))

    hidden, grad_self, grad_neigh = lax.map(wrapped, (feats, tile_weight, tile_src, tile_count, owner_order, cotangent))
    return hidden, jnp.sum(grad_self, axis=0), jnp.sum(grad_neigh, axis=0)
```

```python
import jax
import jax.numpy as jnp
from jax import lax
from jax.sharding import PartitionSpec as P


def transposed_product(left, right):
    return lax.dot_general(
        left, right, (((0,), (0,)), ((), ())), preferred_element_type=jnp.float32
    )


def exchange(value, axis, size, flip):
    return lax.ppermute(value, axis, [(i, i ^ flip) for i in range(size)])


def body(n_feat, n_rep, feats, w_self, w_neigh, bias, tile_weight, tile_src, tile_count, owner_order, cotangent):
    block_rows = tile_weight.shape[3]
    tile_slots = tile_weight.shape[2]
    columns = feats.shape[2]
    hidden_units = w_self.shape[1]
    n_chip = n_feat // 2
    me = lax.axis_index("feat")
    core, chip = me % 2, me // 2
    flips = jnp.arange(n_chip, dtype=jnp.int32)
    places = 2 * (chip ^ flips)
    order = owner_order[0]
    kept, given = order[places + core], order[places + 1 - core]
    blocks = jnp.concatenate([given, kept])

    by_block = feats[0].reshape(-1, block_rows, columns)
    in_use = jnp.arange(tile_slots)[None, :] < tile_count[0][blocks][:, None]
    masked = jnp.where(in_use[:, :, None, None], tile_weight[0][blocks], jnp.zeros((), jnp.bfloat16))
    sources = by_block[tile_src[0][blocks]]
    target_mean = jnp.einsum(
        "bkij,bkjc->bic", masked, sources, preferred_element_type=jnp.float32
    ).astype(jnp.bfloat16)
    target_rows = by_block[blocks]
    both = jnp.concatenate([target_rows, target_mean], axis=2).reshape(-1, 2 * columns)
    weights = jnp.concatenate([w_self, w_neigh], axis=0)
    half = n_chip * block_rows
    partial_sums = jnp.dot(both, weights, preferred_element_type=jnp.float32)

    from_core = exchange(partial_sums[:half].astype(jnp.bfloat16), "feat", n_feat, 1)
    chip_sums = (partial_sums[half:] + from_core.astype(jnp.float32)).reshape(n_chip, block_rows, hidden_units)
    preact = chip_sums[0] + bias
    for j in reversed(range(1, n_chip)):
        got = exchange(chip_sums[j].astype(jnp.bfloat16), "feat", n_feat, 2 * j)
        preact = preact + got.astype(jnp.float32)
    squash = jax.nn.sigmoid(preact)
    hidden = (preact * squash).astype(jnp.bfloat16)
    output_grad = (
        cotangent[0].astype(jnp.float32) * squash * (1.0 + preact * (1.0 - squash))
    ).astype(jnp.bfloat16)

    own = [output_grad] + [exchange(output_grad, "feat", n_feat, 2 * j) for j in range(1, n_chip)]
    own = jnp.concatenate(own, axis=0)
    other = exchange(own, "feat", n_feat, 1)
    grads = transposed_product(both[half:], own) + transposed_product(both[:half], other)

    flip = 1
    while flip < n_rep:
        sent = lax.optimization_barrier(grads.astype(jnp.bfloat16))
        got = exchange(sent, "rep", n_rep, flip)
        grads = sent.astype(jnp.float32) + got.astype(jnp.float32)
        flip *= 2
    return (hidden[None], grads[:columns], grads[columns:])


def solution(mesh):
    n_feat, n_rep = mesh.shape["feat"], mesh.shape["rep"]

    def local(*args):
        return body(n_feat, n_rep, *args)

    in_specs = (
        P("rep", None, "feat"),
        P("feat", None),
        P("feat", None),
        P(),
        P("rep", None, None, None, None),
        P("rep", None, None),
        P("rep", None),
        P("rep", None),
        P("rep", "feat", None),
    )
    out_specs = (P("rep", "feat", None), P("feat", None), P("feat", None))
    return jax.shard_map(local, mesh=mesh, in_specs=in_specs, out_specs=out_specs, check_vma=False)
```

```python
import functools

import jax
import jax.numpy as jnp
from jax import lax
from jax.experimental import pallas as pl
from jax.experimental.pallas import tpu as pltpu
from jax.sharding import PartitionSpec as P


def transposed_product(left, right):
    return lax.dot_general(
        left, right, (((0,), (0,)), ((), ())), preferred_element_type=jnp.float32
    )


def exchange(value, axis, size, flip):
    return lax.ppermute(value, axis, [(i, i ^ flip) for i in range(size)])


def project_blocks(core_flip, order, tile_src, tile_count, feats, tiles, w_self, w_neigh, rows_out, sums_out):
    block_rows = tiles.shape[2]
    tile_slots = tiles.shape[1]
    n_chip = rows_out.shape[0] // block_rows
    me = lax.axis_index("feat")
    weights = jnp.concatenate([w_self[...], w_neigh[...]], axis=0)

    def block_of(index):
        return feats[pl.ds(pl.multiple_of(index * block_rows, block_rows), block_rows), :]

    for j in range(n_chip):
        block = order[0, me ^ (2 * j + core_flip)]
        here = pl.ds(j * block_rows, block_rows)
        used = []
        sources = []
        for k in range(tile_slots):
            tile = tiles[block, k]
            used.append(jnp.where(k < tile_count[0, block], tile, jnp.zeros_like(tile)))
            sources.append(block_of(tile_src[k, 0, block]))
        mean = jnp.dot(
            jnp.concatenate(used, axis=1), jnp.concatenate(sources, axis=0), preferred_element_type=jnp.float32
        ).astype(jnp.bfloat16)
        rows = jnp.concatenate([block_of(block), mean], axis=1)
        rows_out[here, :] = rows
        sums_out[here, :] = jnp.dot(rows, weights, preferred_element_type=jnp.float32).astype(sums_out.dtype)


def load_and_project(*refs):
    loaded_from, rows_out, sums_out, loaded, sems = refs[:7], refs[7], refs[8], refs[9:16], refs[16]
    copies = []
    for i, (source, target) in enumerate(zip(loaded_from, loaded)):
        source = source.at[0] if len(source.shape) > len(target.shape) else source
        copies.append(pltpu.make_async_copy(source, target, sems.at[i]))
        copies[-1].start()
    for copy in copies:
        copy.wait()
    project_blocks(1, *loaded, rows_out, sums_out)


def body(n_feat, n_rep, feats, w_self, w_neigh, bias, tile_weight, tile_src, tile_count, owner_order, cotangent):
    block_rows = tile_weight.shape[3]
    tile_slots = tile_weight.shape[2]
    columns = feats.shape[2]
    hidden_units = w_self.shape[1]
    n_chip = n_feat // 2
    rows = n_chip * block_rows
    tiles_of_slot = jnp.transpose(tile_src, (2, 0, 1))

    operands = (owner_order, tiles_of_slot, tile_count, feats, tile_weight, w_self, w_neigh)
    smem, vmem = pl.BlockSpec(memory_space=pltpu.SMEM), pl.BlockSpec(memory_space=pltpu.VMEM)
    loaded_specs = (smem,) * 3 + (vmem,) * 4
    loaded_shapes = tuple(
        jax.ShapeDtypeStruct(a.shape if i < 3 or i > 4 else a.shape[1:], a.dtype) for i, a in enumerate(operands)
    )
    params = dict(
        compiler_params=pltpu.CompilerParams(vmem_limit_bytes=32 * 1024 * 1024),
        cost_estimate=pl.CostEstimate(
            flops=2 * rows * (tile_slots * block_rows * columns + 2 * columns * hidden_units),
            bytes_accessed=feats.size * 2 + tile_weight.size + rows * 8 * columns,
            transcendentals=0,
        ),
    )

    def results(dtype):
        return (
            jax.ShapeDtypeStruct((rows, 2 * columns), jnp.bfloat16),
            jax.ShapeDtypeStruct((rows, hidden_units), dtype),
        )

    operands = tuple(pltpu.with_memory_space_constraint(a, pltpu.HBM) for a in operands)
    given_rows, given, *loaded = pl.pallas_call(
        load_and_project,
        out_shape=results(jnp.bfloat16) + loaded_shapes,
        in_specs=[pl.BlockSpec(memory_space=pltpu.HBM)] * 7,
        out_specs=(vmem,) * 2 + loaded_specs,
        scratch_shapes=[pltpu.SemaphoreType.DMA((7,))],
        **params,
    )(*operands)
    kept_rows, kept = pl.pallas_call(
        functools.partial(project_blocks, 0),
        out_shape=results(jnp.float32),
        in_specs=loaded_specs,
        out_specs=(vmem,) * 2,
        **params,
    )(*loaded)

    from_core = exchange(given, "feat", n_feat, 1)
    chip_sums = (kept + from_core.astype(jnp.float32)).reshape(n_chip, block_rows, hidden_units)
    preact = chip_sums[0] + bias
    for j in reversed(range(1, n_chip)):
        got = exchange(chip_sums[j].astype(jnp.bfloat16), "feat", n_feat, 2 * j)
        preact = preact + got.astype(jnp.float32)
    squash = jax.nn.sigmoid(preact)
    output_grad = (
        cotangent[0].astype(jnp.float32) * squash * (1.0 + preact * (1.0 - squash))
    ).astype(jnp.bfloat16)
    preact, output_grad = lax.optimization_barrier((preact, output_grad))
    hidden = jax.nn.silu(preact).astype(jnp.bfloat16)

    own = [output_grad] + [exchange(output_grad, "feat", n_feat, 2 * j) for j in range(1, n_chip)]
    own = jnp.concatenate(own, axis=0)
    other = exchange(own, "feat", n_feat, 1)
    grads = transposed_product(kept_rows, own) + transposed_product(given_rows, other)

    flip = 1
    while flip < n_rep:
        sent = lax.optimization_barrier(grads.astype(jnp.bfloat16))
        got = exchange(sent, "rep", n_rep, flip)
        grads = sent.astype(jnp.float32) + got.astype(jnp.float32)
        flip = 2 * flip + 1
    return (hidden[None], grads[:columns], grads[columns:])


def solution(mesh):
    n_feat, n_rep = mesh.shape["feat"], mesh.shape["rep"]

    def local(*args):
        return body(n_feat, n_rep, *args)

    in_specs = (
        P("rep", None, "feat"),
        P("feat", None),
        P("feat", None),
        P(),
        P("rep", None, None, None, None),
        P("rep", None, None),
        P("rep", None),
        P("rep", None),
        P("rep", "feat", None),
    )
    out_specs = (P("rep", "feat", None), P("feat", None), P("feat", None))
    return jax.shard_map(local, mesh=mesh, in_specs=in_specs, out_specs=out_specs, check_vma=False)
```

```python
import functools

import jax
import jax.numpy as jnp
from jax import lax
from jax.experimental import pallas as pl
from jax.experimental.pallas import tpu as pltpu
from jax.sharding import PartitionSpec as P


def transposed_product(left, right):
    return lax.dot_general(
        left, right, (((0,), (0,)), ((), ())), preferred_element_type=jnp.float32
    )


def exchange(value, axis, size, flip):
    return lax.ppermute(value, axis, [(i, i ^ flip) for i in range(size)])


def project_blocks(flips, order, tile_src, tile_count, feats, tiles, w_self, w_neigh, rows_out, sums_out):
    block_rows = tiles.shape[2]
    tile_slots = tiles.shape[1]
    me = lax.axis_index("feat")

    def block_of(index):
        return feats[pl.ds(pl.multiple_of(index * block_rows, block_rows), block_rows), :]

    for j, (even, odd) in enumerate(flips):
        block = order[0, me ^ jnp.where(me % 2 == 0, even, odd)]
        mean = jnp.zeros((block_rows, feats.shape[1]), jnp.float32)
        for k in range(tile_slots):
            tile = tiles[block, k]
            used = jnp.where(k < tile_count[0, block], tile, jnp.zeros_like(tile))
            mean += jnp.dot(used, block_of(tile_src[k, 0, block]), preferred_element_type=jnp.float32)
        rows_out[pl.ds(j * block_rows, block_rows), :] = jnp.concatenate(
            [block_of(block), mean.astype(jnp.bfloat16)], axis=1
        )
    weights = jnp.concatenate([w_self[...], w_neigh[...]], axis=0)
    sums_out[...] = jnp.dot(rows_out[...], weights, preferred_element_type=jnp.float32).astype(sums_out.dtype)


def load_and_project(flips, *refs):
    loaded_from, rows_out, sums_out, loaded, sems = refs[:7], refs[7], refs[8], refs[9:16], refs[16]
    copies = []
    for i, (source, target) in enumerate(zip(loaded_from, loaded)):
        source = source.at[0] if len(source.shape) > len(target.shape) else source
        copies.append(pltpu.make_async_copy(source, target, sems.at[i]))
        copies[-1].start()
    for copy in copies:
        copy.wait()
    project_blocks(flips, *loaded, rows_out, sums_out)


def first_products(kept_rows, given_rows, own, partner, early, total_out):
    n = own.shape[0]
    total = transposed_product(kept_rows[pl.ds(0, n), :], own[...])
    total += transposed_product(given_rows[pl.ds(0, n), :], partner[...])
    total_out[...] = total + transposed_product(kept_rows[pl.ds(2 * n, early.shape[0]), :], early[...])


def last_products(total, kept_rows, given_rows, late, others_late, others_early, total_out):
    n = late.shape[0]
    last = transposed_product(kept_rows[pl.ds(n, n), :], late[...])
    last += transposed_product(given_rows[pl.ds(2 * n, others_early.shape[0]), :], others_early[...])
    last += transposed_product(given_rows[pl.ds(n, n), :], others_late[...])
    total_out[...] = (total[...] + last).astype(jnp.bfloat16)


def body(n_feat, n_rep, feats, w_self, w_neigh, bias, tile_weight, tile_src, tile_count, owner_order, cotangent):
    block_rows = tile_weight.shape[3]
    tile_slots = tile_weight.shape[2]
    columns = feats.shape[2]
    hidden_units = w_self.shape[1]
    n_chip = n_feat // 2
    rows = n_chip * block_rows

    def swap_cores(value):
        return exchange(value, "feat", n_feat, 1)

    kept_flips = tuple((2 * j + (j > 0), 2 * j + (j > 0)) for j in range(n_chip))
    given_flips = tuple((odd ^ 1, even ^ 1) for even, odd in kept_flips)
    tiles_of_slot = jnp.transpose(tile_src, (2, 0, 1))

    operands = (owner_order, tiles_of_slot, tile_count, feats, tile_weight, w_self, w_neigh)
    smem, vmem = pl.BlockSpec(memory_space=pltpu.SMEM), pl.BlockSpec(memory_space=pltpu.VMEM)
    loaded_specs = (smem,) * 3 + (vmem,) * 4
    loaded_shapes = tuple(
        jax.ShapeDtypeStruct(a.shape if i < 3 or i > 4 else a.shape[1:], a.dtype) for i, a in enumerate(operands)
    )
    params = dict(
        compiler_params=pltpu.CompilerParams(vmem_limit_bytes=32 * 1024 * 1024),
        cost_estimate=pl.CostEstimate(
            flops=2 * rows * (tile_slots * block_rows * columns + 2 * columns * hidden_units),
            bytes_accessed=feats.size * 2 + tile_weight.size + rows * 8 * columns,
            transcendentals=0,
        ),
    )

    def results(dtype):
        return (
            jax.ShapeDtypeStruct((rows, 2 * columns), jnp.bfloat16),
            jax.ShapeDtypeStruct((rows, hidden_units), dtype),
        )

    operands = tuple(pltpu.with_memory_space_constraint(a, pltpu.HBM) for a in operands)
    given_rows, given, *loaded = pl.pallas_call(
        functools.partial(load_and_project, given_flips),
        out_shape=results(jnp.bfloat16) + loaded_shapes,
        in_specs=[pl.BlockSpec(memory_space=pltpu.HBM)] * 7,
        out_specs=(vmem,) * 2 + loaded_specs,
        scratch_shapes=[pltpu.SemaphoreType.DMA((7,))],
        **params,
    )(*operands)
    kept_rows, kept = pl.pallas_call(
        functools.partial(project_blocks, kept_flips),
        out_shape=results(jnp.float32),
        in_specs=loaded_specs,
        out_specs=(vmem,) * 2,
        **params,
    )(*loaded)

    from_core = swap_cores(given)
    chip_sums = kept + from_core.astype(jnp.float32)
    arrived = [
        exchange(chip_sums[j * block_rows : (j + 1) * block_rows].astype(jnp.bfloat16), "feat", n_feat, 2 * j + 1)
        for j in reversed(range(1, n_chip))
    ]
    preact = chip_sums[:block_rows] + bias
    for got in arrived:
        preact = preact + got.astype(jnp.float32)
    squash = jax.nn.sigmoid(preact)
    output_grad = (
        cotangent[0].astype(jnp.float32) * squash * (1.0 + preact * (1.0 - squash))
    ).astype(jnp.bfloat16)
    preact, output_grad = lax.optimization_barrier((preact, output_grad))
    hidden = jax.nn.silu(preact).astype(jnp.bfloat16)

    received = [exchange(output_grad, "feat", n_feat, 2 * j + 1) for j in range(1, n_chip)]
    partner = swap_cores(output_grad)
    early = jnp.concatenate(received[1:], axis=0)
    early, partner = lax.optimization_barrier((early, partner))
    others_early = swap_cores(early)
    others_late = swap_cores(received[0])
    products = pl.CostEstimate(flops=2 * rows * 2 * columns * hidden_units, bytes_accessed=0, transcendentals=0)
    total = pl.pallas_call(
        first_products,
        out_shape=jax.ShapeDtypeStruct((2 * columns, hidden_units), jnp.float32),
        in_specs=(vmem,) * 5,
        out_specs=vmem,
        compiler_params=params["compiler_params"],
        cost_estimate=products,
    )(kept_rows, given_rows, output_grad, partner, early)
    grads = pl.pallas_call(
        last_products,
        out_shape=jax.ShapeDtypeStruct((2 * columns, hidden_units), jnp.bfloat16),
        in_specs=(vmem,) * 6,
        out_specs=vmem,
        compiler_params=params["compiler_params"],
        cost_estimate=products,
    )(total, kept_rows, given_rows, received[0], others_late, others_early)

    flip = 1
    while flip < n_rep:
        sent = lax.optimization_barrier(grads.astype(jnp.bfloat16))
        got = exchange(sent, "rep", n_rep, flip)
        grads = sent.astype(jnp.float32) + got.astype(jnp.float32)
        flip = 2 * flip + 1
    return (hidden[None], grads[:columns], grads[columns:])


def solution(mesh):
    n_feat, n_rep = mesh.shape["feat"], mesh.shape["rep"]

    def local(*args):
        return body(n_feat, n_rep, *args)

    in_specs = (
        P("rep", None, "feat"),
        P("feat", None),
        P("feat", None),
        P(),
        P("rep", None, None, None, None),
        P("rep", None, None),
        P("rep", None),
        P("rep", None),
        P("rep", "feat", None),
    )
    out_specs = (P("rep", "feat", None), P("feat", None), P("feat", None))
    return jax.shard_map(local, mesh=mesh, in_specs=in_specs, out_specs=out_specs, check_vma=False)
```

```python
import functools

import jax
import jax.numpy as jnp
from jax import lax
from jax.experimental import pallas as pl
from jax.experimental.pallas import tpu as pltpu
from jax.sharding import PartitionSpec as P


def transposed_product(left, right):
    return lax.dot_general(
        left, right, (((0,), (0,)), ((), ())), preferred_element_type=jnp.float32
    )


def exchange(value, axis, size, flip):
    return lax.ppermute(value, axis, [(i, i ^ flip) for i in range(size)])


def copy_all(pairs, sems):
    copies = [pltpu.make_async_copy(source, target, sems.at[i]) for i, (source, target) in enumerate(pairs)]
    for copy in copies:
        copy.start()
    for copy in copies:
        copy.wait()


def project_blocks(flips, order, tile_src, tile_count, feats, tiles, weights, rows_out, sums_out):
    block_rows = tiles.shape[2]
    tile_slots = tiles.shape[1]
    me = lax.axis_index("feat")

    def block_of(index):
        return feats[pl.ds(pl.multiple_of(index * block_rows, block_rows), block_rows), :]

    for j, flip in enumerate(flips):
        block = order[0, me ^ flip]
        mean = jnp.zeros((block_rows, feats.shape[1]), jnp.float32)
        for k in range(tile_slots):
            tile = tiles[block, k]
            used = jnp.where(k < tile_count[0, block], tile, jnp.zeros_like(tile))
            mean += jnp.dot(used, block_of(tile_src[k, 0, block]), preferred_element_type=jnp.float32)
        rows_out[pl.ds(j * block_rows, block_rows), :] = jnp.concatenate(
            [block_of(block), mean.astype(jnp.bfloat16)], axis=1
        )
    sums_out[...] = jnp.dot(rows_out[...], weights[...], preferred_element_type=jnp.float32).astype(sums_out.dtype)


def load_and_project(
    flips, order_hbm, tile_src_hbm, tile_count_hbm, feats_hbm, tiles_hbm, w_self, w_neigh,
    rows_out, sums_out, feats, tiles, weights, order, tile_src, tile_count, sems,
):
    columns = feats.shape[1]
    copy_all(
        (
            (order_hbm, order),
            (tile_src_hbm, tile_src),
            (tile_count_hbm, tile_count),
            (feats_hbm.at[0], feats),
            (tiles_hbm.at[0], tiles),
            (w_self, weights.at[pl.ds(0, columns)]),
            (w_neigh, weights.at[pl.ds(columns, columns)]),
        ),
        sems,
    )
    project_blocks(flips, order, tile_src, tile_count, feats, tiles, weights, rows_out, sums_out)


def project_loaded(
    flips, order_hbm, tile_src_hbm, tile_count_hbm, feats, tiles, weights,
    rows_out, sums_out, order, tile_src, tile_count, sems,
):
    copy_all(((order_hbm, order), (tile_src_hbm, tile_src), (tile_count_hbm, tile_count)), sems)
    project_blocks(flips, order, tile_src, tile_count, feats, tiles, weights, rows_out, sums_out)


def first_products(kept_rows, given_rows, own, partner, early, total_out):
    n = own.shape[0]
    total = transposed_product(kept_rows[pl.ds(0, n), :], own[...])
    total += transposed_product(given_rows[pl.ds(0, n), :], partner[...])
    total_out[...] = total + transposed_product(kept_rows[pl.ds(2 * n, early.shape[0]), :], early[...])


def last_products(total, kept_rows, given_rows, late, others_late, others_early, total_out):
    n = late.shape[0]
    last = transposed_product(kept_rows[pl.ds(n, n), :], late[...])
    last += transposed_product(given_rows[pl.ds(2 * n, others_early.shape[0]), :], others_early[...])
    last += transposed_product(given_rows[pl.ds(n, n), :], others_late[...])
    total_out[...] = (total[...] + last).astype(jnp.bfloat16)


def body(n_feat, n_rep, feats, w_self, w_neigh, bias, tile_weight, tile_src, tile_count, owner_order, cotangent):
    block_rows = tile_weight.shape[3]
    tile_slots = tile_weight.shape[2]
    columns = feats.shape[2]
    hidden_units = w_self.shape[1]
    n_chip = n_feat // 2
    rows = n_chip * block_rows

    def swap_cores(value):
        return exchange(value, "feat", n_feat, 1)

    kept_flips = (0,) + tuple(2 * j + 1 for j in range(1, n_chip))
    given_flips = tuple(flip ^ 1 for flip in kept_flips)
    tiles_of_slot = jnp.transpose(tile_src, (2, 0, 1))

    operands = (owner_order, tiles_of_slot, tile_count, feats, tile_weight, w_self, w_neigh)
    operands = tuple(pltpu.with_memory_space_constraint(a, pltpu.HBM) for a in operands)
    vmem = pl.BlockSpec(memory_space=pltpu.VMEM)
    params = pltpu.CompilerParams(vmem_limit_bytes=32 * 1024 * 1024)
    hbm = pl.BlockSpec(memory_space=pltpu.HBM)
    indices = [pltpu.SMEM(a.shape, jnp.int32) for a in operands[:3]]

    def results(dtype):
        return (
            jax.ShapeDtypeStruct((rows, 2 * columns), jnp.bfloat16),
            jax.ShapeDtypeStruct((rows, hidden_units), dtype),
        )

    estimate = pl.CostEstimate(
        flops=2 * rows * (tile_slots * block_rows * columns + 2 * columns * hidden_units),
        bytes_accessed=feats.size * 2 + tile_weight.size,
        transcendentals=0,
    )
    given_rows, given, *loaded = pl.pallas_call(
        functools.partial(load_and_project, given_flips),
        out_shape=results(jnp.bfloat16)
        + (
            jax.ShapeDtypeStruct(feats.shape[1:], jnp.bfloat16),
            jax.ShapeDtypeStruct(tile_weight.shape[1:], jnp.bfloat16),
            jax.ShapeDtypeStruct((2 * columns, hidden_units), jnp.bfloat16),
        ),
        in_specs=[hbm] * 7,
        out_specs=(vmem,) * 5,
        scratch_shapes=indices + [pltpu.SemaphoreType.DMA((7,))],
        compiler_params=params,
        cost_estimate=estimate,
    )(*operands)
    kept_rows, kept = pl.pallas_call(
        functools.partial(project_loaded, kept_flips),
        out_shape=results(jnp.float32),
        in_specs=[hbm] * 3 + [vmem] * 3,
        out_specs=(vmem,) * 2,
        scratch_shapes=indices + [pltpu.SemaphoreType.DMA((3,))],
        compiler_params=params,
        cost_estimate=estimate,
    )(*operands[:3], *loaded)

    from_core = swap_cores(given)
    chip_sums = kept + from_core.astype(jnp.float32)
    arrived = [
        exchange(chip_sums[j * block_rows : (j + 1) * block_rows].astype(jnp.bfloat16), "feat", n_feat, 2 * j + 1)
        for j in reversed(range(1, n_chip))
    ]
    preact = chip_sums[:block_rows] + bias
    for got in arrived:
        preact = preact + got.astype(jnp.float32)
    squash = jax.nn.sigmoid(preact)
    output_grad = (
        cotangent[0].astype(jnp.float32) * squash * (1.0 + preact * (1.0 - squash))
    ).astype(jnp.bfloat16)
    preact, output_grad = lax.optimization_barrier((preact, output_grad))
    hidden = jax.nn.silu(preact).astype(jnp.bfloat16)

    received = [exchange(output_grad, "feat", n_feat, 2 * j + 1) for j in range(1, n_chip)]
    partner = swap_cores(output_grad)
    early = jnp.concatenate(received[1:], axis=0)
    early, partner = lax.optimization_barrier((early, partner))
    others_early = swap_cores(early)
    others_late = swap_cores(received[0])
    products = pl.CostEstimate(flops=2 * rows * 2 * columns * hidden_units, bytes_accessed=0, transcendentals=0)
    total = pl.pallas_call(
        first_products,
        out_shape=jax.ShapeDtypeStruct((2 * columns, hidden_units), jnp.float32),
        in_specs=(vmem,) * 5,
        out_specs=vmem,
        compiler_params=params,
        cost_estimate=products,
    )(kept_rows, given_rows, output_grad, partner, early)
    grads = pl.pallas_call(
        last_products,
        out_shape=jax.ShapeDtypeStruct((2 * columns, hidden_units), jnp.bfloat16),
        in_specs=(vmem,) * 6,
        out_specs=vmem,
        compiler_params=params,
        cost_estimate=products,
    )(total, kept_rows, given_rows, received[0], others_late, others_early)

    flip = 1
    while flip < n_rep:
        sent = lax.optimization_barrier(grads.astype(jnp.bfloat16))
        got = exchange(sent, "rep", n_rep, flip)
        grads = sent.astype(jnp.float32) + got.astype(jnp.float32)
        flip = 2 * flip + 1
    return (hidden[None], grads[:columns], grads[columns:])


def solution(mesh):
    n_feat, n_rep = mesh.shape["feat"], mesh.shape["rep"]

    def local(*args):
        return body(n_feat, n_rep, *args)

    in_specs = (
        P("rep", None, "feat"),
        P("feat", None),
        P("feat", None),
        P(),
        P("rep", None, None, None, None),
        P("rep", None, None),
        P("rep", None),
        P("rep", None),
        P("rep", "feat", None),
    )
    out_specs = (P("rep", "feat", None), P("feat", None), P("feat", None))
    return jax.shard_map(local, mesh=mesh, in_specs=in_specs, out_specs=out_specs, check_vma=False)
```

```python
import functools

import jax
import jax.numpy as jnp
from jax import lax
from jax.experimental import pallas as pl
from jax.experimental.pallas import tpu as pltpu
from jax.sharding import PartitionSpec as P


def transposed_product(left, right):
    return lax.dot_general(
        left, right, (((0,), (0,)), ((), ())), preferred_element_type=jnp.float32
    )


def exchange(value, axis, size, flip):
    return lax.ppermute(value, axis, [(i, i ^ flip) for i in range(size)])


def copy_all(pairs, sems):
    copies = [pltpu.make_async_copy(source, target, sems.at[i]) for i, (source, target) in enumerate(pairs)]
    for copy in copies:
        copy.start()
    for copy in copies:
        copy.wait()


def project_blocks(flips, order, tile_src, tile_count, feats, tiles, weights, rows_out, sums_out):
    block_rows = tiles.shape[2]
    tile_slots = tiles.shape[1]
    me = lax.axis_index("feat")

    def block_of(index):
        return feats[pl.ds(pl.multiple_of(index * block_rows, block_rows), block_rows), :]

    for j, flip in enumerate(flips):
        block = order[0, me ^ flip]
        mean = jnp.zeros((block_rows, feats.shape[1]), jnp.float32)
        for k in range(tile_slots):
            tile = tiles[block, k]
            used = jnp.where(k < tile_count[0, block], tile, jnp.zeros_like(tile))
            mean += jnp.dot(used, block_of(tile_src[k, 0, block]), preferred_element_type=jnp.float32)
        rows_out[pl.ds(j * block_rows, block_rows), :] = jnp.concatenate(
            [block_of(block), mean.astype(jnp.bfloat16)], axis=1
        )
    sums_out[...] = jnp.dot(rows_out[...], weights[...], preferred_element_type=jnp.float32).astype(sums_out.dtype)


def load_and_project(
    flips, order_hbm, tile_src_hbm, tile_count_hbm, feats_hbm, tiles_hbm, w_self, w_neigh,
    rows_out, sums_out, feats, tiles, weights, order, tile_src, tile_count, sems,
):
    columns = feats.shape[1]
    copy_all(
        (
            (order_hbm, order),
            (tile_src_hbm, tile_src),
            (tile_count_hbm, tile_count),
            (feats_hbm.at[0], feats),
            (tiles_hbm.at[0], tiles),
            (w_self, weights.at[pl.ds(0, columns)]),
            (w_neigh, weights.at[pl.ds(columns, columns)]),
        ),
        sems,
    )
    project_blocks(flips, order, tile_src, tile_count, feats, tiles, weights, rows_out, sums_out)


def project_loaded(
    flips, order_hbm, tile_src_hbm, tile_count_hbm, feats, tiles, weights,
    rows_out, sums_out, order, tile_src, tile_count, sems,
):
    copy_all(((order_hbm, order), (tile_src_hbm, tile_src), (tile_count_hbm, tile_count)), sems)
    project_blocks(flips, order, tile_src, tile_count, feats, tiles, weights, rows_out, sums_out)


def first_products(kept_rows, given_rows, own, partner, early, total_out):
    n = own.shape[0]
    total = transposed_product(kept_rows[pl.ds(0, n), :], own[...])
    total += transposed_product(given_rows[pl.ds(0, n), :], partner[...])
    total_out[...] = total + transposed_product(kept_rows[pl.ds(2 * n, early.shape[0]), :], early[...])


def last_products(total, kept_rows, given_rows, late, others_late, others_early, total_out):
    n = late.shape[0]
    last = transposed_product(kept_rows[pl.ds(n, n), :], late[...])
    last += transposed_product(given_rows[pl.ds(2 * n, others_early.shape[0]), :], others_early[...])
    last += transposed_product(given_rows[pl.ds(n, n), :], others_late[...])
    total_out[...] = (total[...] + last).astype(jnp.bfloat16)


def body(n_feat, n_rep, feats, w_self, w_neigh, bias, tile_weight, tile_src, tile_count, owner_order, cotangent):
    block_rows = tile_weight.shape[3]
    tile_slots = tile_weight.shape[2]
    columns = feats.shape[2]
    hidden_units = w_self.shape[1]
    n_chip = n_feat // 2
    rows = n_chip * block_rows

    def swap_cores(value):
        return exchange(value, "feat", n_feat, 1)

    kept_flips = (0,) + tuple(2 * j + 1 for j in range(1, n_chip))
    given_flips = tuple(flip ^ 1 for flip in kept_flips)
    tiles_of_slot = jnp.transpose(tile_src, (2, 0, 1))

    operands = (owner_order, tiles_of_slot, tile_count, feats, tile_weight, w_self, w_neigh)
    operands = tuple(pltpu.with_memory_space_constraint(a, pltpu.HBM) for a in operands)
    vmem = pl.BlockSpec(memory_space=pltpu.VMEM)
    params = pltpu.CompilerParams(vmem_limit_bytes=32 * 1024 * 1024)
    hbm = pl.BlockSpec(memory_space=pltpu.HBM)
    indices = [pltpu.SMEM(a.shape, jnp.int32) for a in operands[:3]]

    def results(dtype):
        return (
            jax.ShapeDtypeStruct((rows, 2 * columns), jnp.bfloat16),
            jax.ShapeDtypeStruct((rows, hidden_units), dtype),
        )

    estimate = pl.CostEstimate(
        flops=2 * rows * (tile_slots * block_rows * columns + 2 * columns * hidden_units),
        bytes_accessed=feats.size * 2 + tile_weight.size,
        transcendentals=0,
    )
    given_rows, given, *loaded = pl.pallas_call(
        functools.partial(load_and_project, given_flips),
        out_shape=results(jnp.bfloat16)
        + (
            jax.ShapeDtypeStruct(feats.shape[1:], jnp.bfloat16),
            jax.ShapeDtypeStruct(tile_weight.shape[1:], jnp.bfloat16),
            jax.ShapeDtypeStruct((2 * columns, hidden_units), jnp.bfloat16),
        ),
        in_specs=[hbm] * 7,
        out_specs=(vmem,) * 5,
        scratch_shapes=indices + [pltpu.SemaphoreType.DMA((7,))],
        compiler_params=params,
        cost_estimate=estimate,
    )(*operands)
    kept_rows, kept = pl.pallas_call(
        functools.partial(project_loaded, kept_flips),
        out_shape=results(jnp.float32),
        in_specs=[hbm] * 3 + [vmem] * 3,
        out_specs=(vmem,) * 2,
        scratch_shapes=indices + [pltpu.SemaphoreType.DMA((3,))],
        compiler_params=params,
        cost_estimate=estimate,
    )(*operands[:3], *loaded)

    from_core = swap_cores(given)
    chip_sums = kept + from_core.astype(jnp.float32)
    arrived = [
        exchange(chip_sums[j * block_rows : (j + 1) * block_rows].astype(jnp.bfloat16), "feat", n_feat, 2 * j + 1)
        for j in reversed(range(1, n_chip))
    ]
    preact = chip_sums[:block_rows] + bias
    for got in arrived:
        preact = preact + got.astype(jnp.float32)
    squash = jax.nn.sigmoid(preact)
    output_grad = (
        cotangent[0].astype(jnp.float32) * squash * (1.0 + preact * (1.0 - squash))
    ).astype(jnp.bfloat16)
    preact, output_grad = lax.optimization_barrier((preact, output_grad))
    hidden = jax.nn.silu(preact).astype(jnp.bfloat16)

    received = [exchange(output_grad, "feat", n_feat, 2 * j + 1) for j in range(1, n_chip)]
    partner = swap_cores(output_grad)
    early = jnp.concatenate(received[1:], axis=0)
    early, partner = lax.optimization_barrier((early, partner))
    others_early = swap_cores(early)
    others_late = swap_cores(received[0])
    products = pl.CostEstimate(flops=2 * rows * 2 * columns * hidden_units, bytes_accessed=0, transcendentals=0)
    total = pl.pallas_call(
        first_products,
        out_shape=jax.ShapeDtypeStruct((2 * columns, hidden_units), jnp.float32),
        in_specs=(vmem,) * 5,
        out_specs=vmem,
        compiler_params=params,
        cost_estimate=products,
    )(kept_rows, given_rows, output_grad, partner, early)
    grads = pl.pallas_call(
        last_products,
        out_shape=jax.ShapeDtypeStruct((2 * columns, hidden_units), jnp.bfloat16),
        in_specs=(vmem,) * 6,
        out_specs=vmem,
        compiler_params=params,
        cost_estimate=products,
    )(total, kept_rows, given_rows, received[0], others_late, others_early)

    n_flips = n_rep.bit_length() - 1
    for step in range(n_flips):
        flips = (2 ** (n_flips - 1 - step), 2 ** (step + 1) - 1)
        sent = lax.optimization_barrier(grads.astype(jnp.bfloat16))
        pairs = [(f * n_rep + r, f * n_rep + (r ^ flips[f % 2])) for f in range(n_feat) for r in range(n_rep)]
        got = lax.ppermute(sent, ("feat", "rep"), pairs)
        grads = sent.astype(jnp.float32) + got.astype(jnp.float32)
    return (hidden[None], grads[:columns], grads[columns:])


def solution(mesh):
    n_feat, n_rep = mesh.shape["feat"], mesh.shape["rep"]

    def local(*args):
        return body(n_feat, n_rep, *args)

    in_specs = (
        P("rep", None, "feat"),
        P("feat", None),
        P("feat", None),
        P(),
        P("rep", None, None, None, None),
        P("rep", None, None),
        P("rep", None),
        P("rep", None),
        P("rep", "feat", None),
    )
    out_specs = (P("rep", "feat", None), P("feat", None), P("feat", None))
    return jax.shard_map(local, mesh=mesh, in_specs=in_specs, out_specs=out_specs, check_vma=False)
```

```python
import functools

import jax
import jax.numpy as jnp
from jax import lax
from jax.experimental import pallas as pl
from jax.experimental.pallas import tpu as pltpu
from jax.sharding import PartitionSpec as P


def transposed_product(left, right):
    return lax.dot_general(
        left, right, (((0,), (0,)), ((), ())), preferred_element_type=jnp.float32
    )


def exchange(value, axis, size, flip):
    return lax.ppermute(value, axis, [(i, i ^ flip) for i in range(size)])


def copy_all(pairs, sems):
    copies = [pltpu.make_async_copy(source, target, sems.at[i]) for i, (source, target) in enumerate(pairs)]
    for copy in copies:
        copy.start()
    for copy in copies:
        copy.wait()


def project_blocks(flips, order, tile_src, tile_count, feats, tiles, weights, rows_out, sums_out):
    block_rows = tiles.shape[2]
    tile_slots = tiles.shape[1]
    me = lax.axis_index("feat")

    def block_of(index):
        return feats[pl.ds(pl.multiple_of(index * block_rows, block_rows), block_rows), :]

    for j, flip in enumerate(flips):
        block = order[0, me ^ flip]
        mean = jnp.zeros((block_rows, feats.shape[1]), jnp.float32)
        for k in range(tile_slots):
            tile = tiles[block, k]
            used = jnp.where(k < tile_count[0, block], tile, jnp.zeros_like(tile))
            mean += jnp.dot(used, block_of(tile_src[k, 0, block]), preferred_element_type=jnp.float32)
        rows_out[pl.ds(j * block_rows, block_rows), :] = jnp.concatenate(
            [block_of(block), mean.astype(jnp.bfloat16)], axis=1
        )
    sums_out[...] = jnp.dot(rows_out[...], weights[...], preferred_element_type=jnp.float32).astype(sums_out.dtype)


def load_and_project(
    flips, order_hbm, tile_src_hbm, tile_count_hbm, feats_hbm, tiles_hbm, w_self, w_neigh,
    rows_out, sums_out, feats, tiles, weights, order, tile_src, tile_count, sems,
):
    columns = feats.shape[1]
    copy_all(
        (
            (order_hbm, order),
            (tile_src_hbm, tile_src),
            (tile_count_hbm, tile_count),
            (feats_hbm.at[0], feats),
            (tiles_hbm.at[0], tiles),
            (w_self, weights.at[pl.ds(0, columns)]),
            (w_neigh, weights.at[pl.ds(columns, columns)]),
        ),
        sems,
    )
    project_blocks(flips, order, tile_src, tile_count, feats, tiles, weights, rows_out, sums_out)


def project_loaded(
    flips, order_hbm, tile_src_hbm, tile_count_hbm, feats, tiles, weights,
    rows_out, sums_out, order, tile_src, tile_count, sems,
):
    copy_all(((order_hbm, order), (tile_src_hbm, tile_src), (tile_count_hbm, tile_count)), sems)
    project_blocks(flips, order, tile_src, tile_count, feats, tiles, weights, rows_out, sums_out)


def first_products(kept_rows, given_rows, own, partner, early, total_out):
    n = own.shape[0]
    total = transposed_product(kept_rows[pl.ds(0, n), :], own[...])
    total += transposed_product(given_rows[pl.ds(0, n), :], partner[...])
    total_out[...] = total + transposed_product(kept_rows[pl.ds(2 * n, early.shape[0]), :], early[...])


def last_products(total, kept_rows, given_rows, late, others_late, others_early, total_out):
    n = late.shape[0]
    last = transposed_product(kept_rows[pl.ds(n, n), :], late[...])
    last += transposed_product(given_rows[pl.ds(2 * n, others_early.shape[0]), :], others_early[...])
    last += transposed_product(given_rows[pl.ds(n, n), :], others_late[...])
    total_out[...] = (total[...] + last).astype(jnp.bfloat16)


def body(n_feat, n_rep, feats, w_self, w_neigh, bias, tile_weight, tile_src, tile_count, owner_order, cotangent):
    block_rows = tile_weight.shape[3]
    tile_slots = tile_weight.shape[2]
    columns = feats.shape[2]
    hidden_units = w_self.shape[1]
    n_chip = n_feat // 2
    rows = n_chip * block_rows

    def swap_cores(value):
        return exchange(value, "feat", n_feat, 1)

    kept_flips = (0,) + tuple(2 * j + 1 for j in range(1, n_chip))
    given_flips = tuple(flip ^ 1 for flip in kept_flips)
    tiles_of_slot = jnp.transpose(tile_src, (2, 0, 1))

    operands = (owner_order, tiles_of_slot, tile_count, feats, tile_weight, w_self, w_neigh)
    operands = tuple(pltpu.with_memory_space_constraint(a, pltpu.HBM) for a in operands)
    vmem = pl.BlockSpec(memory_space=pltpu.VMEM)
    params = pltpu.CompilerParams(vmem_limit_bytes=32 * 1024 * 1024)
    hbm = pl.BlockSpec(memory_space=pltpu.HBM)
    indices = [pltpu.SMEM(a.shape, jnp.int32) for a in operands[:3]]

    def results(dtype):
        return (
            jax.ShapeDtypeStruct((rows, 2 * columns), jnp.bfloat16),
            jax.ShapeDtypeStruct((rows, hidden_units), dtype),
        )

    estimate = pl.CostEstimate(
        flops=2 * rows * (tile_slots * block_rows * columns + 2 * columns * hidden_units),
        bytes_accessed=feats.size * 2 + tile_weight.size,
        transcendentals=0,
    )
    given_rows, given, *loaded = pl.pallas_call(
        functools.partial(load_and_project, given_flips),
        out_shape=results(jnp.bfloat16)
        + (
            jax.ShapeDtypeStruct(feats.shape[1:], jnp.bfloat16),
            jax.ShapeDtypeStruct(tile_weight.shape[1:], jnp.bfloat16),
            jax.ShapeDtypeStruct((2 * columns, hidden_units), jnp.bfloat16),
        ),
        in_specs=[hbm] * 7,
        out_specs=(vmem,) * 5,
        scratch_shapes=indices + [pltpu.SemaphoreType.DMA((7,))],
        compiler_params=params,
        cost_estimate=estimate,
    )(*operands)
    kept_rows, kept = pl.pallas_call(
        functools.partial(project_loaded, kept_flips),
        out_shape=results(jnp.float32),
        in_specs=[hbm] * 3 + [vmem] * 3,
        out_specs=(vmem,) * 2,
        scratch_shapes=indices + [pltpu.SemaphoreType.DMA((3,))],
        compiler_params=params,
        cost_estimate=estimate,
    )(*operands[:3], *loaded)

    from_core = swap_cores(given)
    chip_sums = kept + from_core.astype(jnp.float32)
    arrived = [
        exchange(chip_sums[j * block_rows : (j + 1) * block_rows].astype(jnp.bfloat16), "feat", n_feat, 2 * j + 1)
        for j in sorted(range(1, n_chip), key=lambda j: (j.bit_count(), -j))
    ]
    preact = chip_sums[:block_rows] + bias
    for got in arrived:
        preact = preact + got.astype(jnp.float32)
    squash = jax.nn.sigmoid(preact)
    output_grad = (
        cotangent[0].astype(jnp.float32) * squash * (1.0 + preact * (1.0 - squash))
    ).astype(jnp.bfloat16)
    preact, output_grad = lax.optimization_barrier((preact, output_grad))
    hidden = jax.nn.silu(preact).astype(jnp.bfloat16)

    received = [exchange(output_grad, "feat", n_feat, 2 * j + 1) for j in range(1, n_chip)]
    partner = swap_cores(output_grad)
    early = jnp.concatenate(received[1:], axis=0)
    early, partner = lax.optimization_barrier((early, partner))
    others_early = swap_cores(early)
    others_late = swap_cores(received[0])
    products = pl.CostEstimate(flops=2 * rows * 2 * columns * hidden_units, bytes_accessed=0, transcendentals=0)
    total = pl.pallas_call(
        first_products,
        out_shape=jax.ShapeDtypeStruct((2 * columns, hidden_units), jnp.float32),
        in_specs=(vmem,) * 5,
        out_specs=vmem,
        compiler_params=params,
        cost_estimate=products,
    )(kept_rows, given_rows, output_grad, partner, early)
    grads = pl.pallas_call(
        last_products,
        out_shape=jax.ShapeDtypeStruct((2 * columns, hidden_units), jnp.bfloat16),
        in_specs=(vmem,) * 6,
        out_specs=vmem,
        compiler_params=params,
        cost_estimate=products,
    )(total, kept_rows, given_rows, received[0], others_late, others_early)

    n_flips = n_rep.bit_length() - 1
    for step in range(n_flips):
        flips = (2 ** (n_flips - 1 - step), 2 ** (step + 1) - 1)
        sent = lax.optimization_barrier(grads.astype(jnp.bfloat16))
        pairs = [(f * n_rep + r, f * n_rep + (r ^ flips[f % 2])) for f in range(n_feat) for r in range(n_rep)]
        got = lax.ppermute(sent, ("feat", "rep"), pairs)
        grads = sent.astype(jnp.float32) + got.astype(jnp.float32)
    return (hidden[None], grads[:columns], grads[columns:])


def solution(mesh):
    n_feat, n_rep = mesh.shape["feat"], mesh.shape["rep"]

    def local(*args):
        return body(n_feat, n_rep, *args)

    in_specs = (
        P("rep", None, "feat"),
        P("feat", None),
        P("feat", None),
        P(),
        P("rep", None, None, None, None),
        P("rep", None, None),
        P("rep", None),
        P("rep", None),
        P("rep", "feat", None),
    )
    out_specs = (P("rep", "feat", None), P("feat", None), P("feat", None))
    return jax.shard_map(local, mesh=mesh, in_specs=in_specs, out_specs=out_specs, check_vma=False)
```

```python
import functools

import jax
import jax.numpy as jnp
from jax import lax
from jax.experimental import pallas as pl
from jax.experimental.pallas import tpu as pltpu
from jax.sharding import PartitionSpec as P


def transposed_product(left, right):
    return lax.dot_general(
        left, right, (((0,), (0,)), ((), ())), preferred_element_type=jnp.float32
    )


def exchange(value, axis, size, flip):
    return lax.ppermute(value, axis, [(i, i ^ flip) for i in range(size)])


def copy_all(pairs, sems):
    copies = [pltpu.make_async_copy(source, target, sems.at[i]) for i, (source, target) in enumerate(pairs)]
    for copy in copies:
        copy.start()
    for copy in copies:
        copy.wait()


def project_blocks(flips, order, tile_src, tile_count, feats, tiles, weights, rows_out, sums_out):
    block_rows = tiles.shape[2]
    tile_slots = tiles.shape[1]
    me = lax.axis_index("feat")

    def block_of(index):
        return feats[pl.ds(pl.multiple_of(index * block_rows, block_rows), block_rows), :]

    for j, flip in enumerate(flips):
        block = order[0, me ^ flip]
        mean = jnp.zeros((block_rows, feats.shape[1]), jnp.float32)
        for k in range(tile_slots):
            tile = tiles[block, k]
            used = jnp.where(k < tile_count[0, block], tile, jnp.zeros_like(tile))
            mean += jnp.dot(used, block_of(tile_src[k, 0, block]), preferred_element_type=jnp.float32)
        rows_out[pl.ds(j * block_rows, block_rows), :] = jnp.concatenate(
            [block_of(block), mean.astype(jnp.bfloat16)], axis=1
        )
    sums_out[...] = jnp.dot(rows_out[...], weights[...], preferred_element_type=jnp.float32).astype(sums_out.dtype)


def load_and_project(
    flips, order_hbm, tile_src_hbm, tile_count_hbm, feats_hbm, tiles_hbm, w_self, w_neigh,
    rows_out, sums_out, feats, tiles, weights, order, tile_src, tile_count, sems,
):
    columns = feats.shape[1]
    copy_all(
        (
            (order_hbm, order),
            (tile_src_hbm, tile_src),
            (tile_count_hbm, tile_count),
            (feats_hbm.at[0], feats),
            (tiles_hbm.at[0], tiles),
            (w_self, weights.at[pl.ds(0, columns)]),
            (w_neigh, weights.at[pl.ds(columns, columns)]),
        ),
        sems,
    )
    project_blocks(flips, order, tile_src, tile_count, feats, tiles, weights, rows_out, sums_out)


def project_loaded(
    flips, order_hbm, tile_src_hbm, tile_count_hbm, feats, tiles, weights,
    rows_out, sums_out, order, tile_src, tile_count, sems,
):
    copy_all(((order_hbm, order), (tile_src_hbm, tile_src), (tile_count_hbm, tile_count)), sems)
    project_blocks(flips, order, tile_src, tile_count, feats, tiles, weights, rows_out, sums_out)


def first_products(kept_rows, given_rows, own, partner, early, total_out):
    n = own.shape[0]
    total = transposed_product(kept_rows[pl.ds(0, n), :], own[...])
    total += transposed_product(given_rows[pl.ds(0, n), :], partner[...])
    total_out[...] = total + transposed_product(kept_rows[pl.ds(2 * n, early.shape[0]), :], early[...])


def last_products(total, kept_rows, given_rows, late, others_late, others_early, total_out):
    n = late.shape[0]
    last = transposed_product(kept_rows[pl.ds(n, n), :], late[...])
    last += transposed_product(given_rows[pl.ds(2 * n, others_early.shape[0]), :], others_early[...])
    last += transposed_product(given_rows[pl.ds(n, n), :], others_late[...])
    total_out[...] = (total[...] + last).astype(jnp.bfloat16)


def body(n_feat, n_rep, feats, w_self, w_neigh, bias, tile_weight, tile_src, tile_count, owner_order, cotangent):
    block_rows = tile_weight.shape[3]
    tile_slots = tile_weight.shape[2]
    columns = feats.shape[2]
    hidden_units = w_self.shape[1]
    n_chip = n_feat // 2
    rows = n_chip * block_rows

    def swap_cores(value):
        return exchange(value, "feat", n_feat, 1)

    chips = [0, 1] + list(range(n_chip - 1, 1, -1))
    kept_flips = (0,) + tuple(2 * chip + 1 for chip in chips[1:])
    given_flips = tuple(flip ^ 1 for flip in kept_flips)
    tiles_of_slot = jnp.transpose(tile_src, (2, 0, 1))

    operands = (owner_order, tiles_of_slot, tile_count, feats, tile_weight, w_self, w_neigh)
    operands = tuple(pltpu.with_memory_space_constraint(a, pltpu.HBM) for a in operands)
    vmem = pl.BlockSpec(memory_space=pltpu.VMEM)
    params = pltpu.CompilerParams(vmem_limit_bytes=32 * 1024 * 1024)
    hbm = pl.BlockSpec(memory_space=pltpu.HBM)
    indices = [pltpu.SMEM(a.shape, jnp.int32) for a in operands[:3]]

    def results(dtype):
        return (
            jax.ShapeDtypeStruct((rows, 2 * columns), jnp.bfloat16),
            jax.ShapeDtypeStruct((rows, hidden_units), dtype),
        )

    estimate = pl.CostEstimate(
        flops=2 * rows * (tile_slots * block_rows * columns + 2 * columns * hidden_units),
        bytes_accessed=feats.size * 2 + tile_weight.size,
        transcendentals=0,
    )
    given_rows, given, *loaded = pl.pallas_call(
        functools.partial(load_and_project, given_flips),
        out_shape=results(jnp.bfloat16)
        + (
            jax.ShapeDtypeStruct(feats.shape[1:], jnp.bfloat16),
            jax.ShapeDtypeStruct(tile_weight.shape[1:], jnp.bfloat16),
            jax.ShapeDtypeStruct((2 * columns, hidden_units), jnp.bfloat16),
        ),
        in_specs=[hbm] * 7,
        out_specs=(vmem,) * 5,
        scratch_shapes=indices + [pltpu.SemaphoreType.DMA((7,))],
        compiler_params=params,
        cost_estimate=estimate,
    )(*operands)
    kept_rows, kept = pl.pallas_call(
        functools.partial(project_loaded, kept_flips),
        out_shape=results(jnp.float32),
        in_specs=[hbm] * 3 + [vmem] * 3,
        out_specs=(vmem,) * 2,
        scratch_shapes=indices + [pltpu.SemaphoreType.DMA((3,))],
        compiler_params=params,
        cost_estimate=estimate,
    )(*operands[:3], *loaded)

    from_core = swap_cores(given)
    chip_sums = kept + from_core.astype(jnp.float32)
    arrived = [
        exchange(chip_sums[j * block_rows : (j + 1) * block_rows].astype(jnp.bfloat16), "feat", n_feat, kept_flips[j])
        for j in sorted(range(1, n_chip), key=lambda j: (chips[j].bit_count(), -chips[j]))
    ]
    preact = chip_sums[:block_rows] + bias
    for got in arrived:
        preact = preact + got.astype(jnp.float32)
    squash = jax.nn.sigmoid(preact)
    output_grad = (
        cotangent[0].astype(jnp.float32) * squash * (1.0 + preact * (1.0 - squash))
    ).astype(jnp.bfloat16)
    preact, output_grad = lax.optimization_barrier((preact, output_grad))
    hidden = jax.nn.silu(preact).astype(jnp.bfloat16)

    received = [exchange(output_grad, "feat", n_feat, kept_flips[j]) for j in range(1, n_chip)]
    partner = swap_cores(output_grad)
    early = jnp.concatenate(received[1:], axis=0)
    early, partner = lax.optimization_barrier((early, partner))
    others_early = swap_cores(early)
    others_late = swap_cores(received[0])
    products = pl.CostEstimate(flops=2 * rows * 2 * columns * hidden_units, bytes_accessed=0, transcendentals=0)
    total = pl.pallas_call(
        first_products,
        out_shape=jax.ShapeDtypeStruct((2 * columns, hidden_units), jnp.float32),
        in_specs=(vmem,) * 5,
        out_specs=vmem,
        compiler_params=params,
        cost_estimate=products,
    )(kept_rows, given_rows, output_grad, partner, early)
    grads = pl.pallas_call(
        last_products,
        out_shape=jax.ShapeDtypeStruct((2 * columns, hidden_units), jnp.bfloat16),
        in_specs=(vmem,) * 6,
        out_specs=vmem,
        compiler_params=params,
        cost_estimate=products,
    )(total, kept_rows, given_rows, received[0], others_late, others_early)

    n_flips = n_rep.bit_length() - 1
    for step in range(n_flips):
        flips = (2 ** (n_flips - 1 - step), 2 ** (step + 1) - 1)
        sent = lax.optimization_barrier(grads.astype(jnp.bfloat16))
        pairs = [(f * n_rep + r, f * n_rep + (r ^ flips[f % 2])) for f in range(n_feat) for r in range(n_rep)]
        got = lax.ppermute(sent, ("feat", "rep"), pairs)
        grads = sent.astype(jnp.float32) + got.astype(jnp.float32)
    return (hidden[None], grads[:columns], grads[columns:])


def solution(mesh):
    n_feat, n_rep = mesh.shape["feat"], mesh.shape["rep"]

    def local(*args):
        return body(n_feat, n_rep, *args)

    in_specs = (
        P("rep", None, "feat"),
        P("feat", None),
        P("feat", None),
        P(),
        P("rep", None, None, None, None),
        P("rep", None, None),
        P("rep", None),
        P("rep", None),
        P("rep", "feat", None),
    )
    out_specs = (P("rep", "feat", None), P("feat", None), P("feat", None))
    return jax.shard_map(local, mesh=mesh, in_specs=in_specs, out_specs=out_specs, check_vma=False)
```

```python
import functools

import jax
import jax.numpy as jnp
from jax import lax
from jax.experimental import pallas as pl
from jax.experimental.pallas import tpu as pltpu
from jax.sharding import PartitionSpec as P


def transposed_product(left, right):
    return lax.dot_general(
        left, right, (((0,), (0,)), ((), ())), preferred_element_type=jnp.float32
    )


def exchange(value, axis, size, flip):
    return lax.ppermute(value, axis, [(i, i ^ flip) for i in range(size)])


def start_all(pairs, sems):
    copies = [pltpu.make_async_copy(source, target, sems.at[i]) for i, (source, target) in enumerate(pairs)]
    for copy in copies:
        copy.start()
    return copies


def copy_all(pairs, sems):
    for copy in start_all(pairs, sems):
        copy.wait()


def project_blocks(flips, order, tile_src, tile_count, feats, tiles, weights, rows_out, sums_out, tiles_copy=None):
    block_rows = tiles.shape[2]
    tile_slots = tiles.shape[1]
    me = lax.axis_index("feat")

    def block_of(index):
        return feats[pl.ds(pl.multiple_of(index * block_rows, block_rows), block_rows), :]

    columns = feats.shape[1]
    for j, flip in enumerate(flips):
        rows_out[pl.ds(j * block_rows, block_rows), pl.ds(0, columns)] = block_of(order[0, me ^ flip])
    if tiles_copy is not None:
        own = jnp.dot(rows_out[:, pl.ds(0, columns)], weights[pl.ds(0, columns), :], preferred_element_type=jnp.float32)
        tiles_copy.wait()
    for j, flip in enumerate(flips):
        block = order[0, me ^ flip]
        mean = jnp.zeros((block_rows, columns), jnp.float32)
        for k in range(tile_slots):
            tile = tiles[block, k]
            used = jnp.where(k < tile_count[0, block], tile, jnp.zeros_like(tile))
            mean += jnp.dot(used, block_of(tile_src[k, 0, block]), preferred_element_type=jnp.float32)
        rows_out[pl.ds(j * block_rows, block_rows), pl.ds(columns, columns)] = mean.astype(jnp.bfloat16)
    if tiles_copy is not None:
        sums = own + jnp.dot(
            rows_out[:, pl.ds(columns, columns)], weights[pl.ds(columns, columns), :], preferred_element_type=jnp.float32
        )
    else:
        sums = jnp.dot(rows_out[...], weights[...], preferred_element_type=jnp.float32)
    sums_out[...] = sums.astype(sums_out.dtype)


def load_and_project(
    flips, order_hbm, tile_src_hbm, tile_count_hbm, feats_hbm, tiles_hbm, w_self, w_neigh,
    rows_out, sums_out, feats, tiles, weights, order, tile_src, tile_count, sems,
):
    columns = feats.shape[1]
    copies = start_all(
        (
            (order_hbm, order),
            (tile_src_hbm, tile_src),
            (tile_count_hbm, tile_count),
            (feats_hbm.at[0], feats),
            (w_self, weights.at[pl.ds(0, columns)]),
            (w_neigh, weights.at[pl.ds(columns, columns)]),
            (tiles_hbm.at[0], tiles),
        ),
        sems,
    )
    for copy in copies[:-1]:
        copy.wait()
    project_blocks(flips, order, tile_src, tile_count, feats, tiles, weights, rows_out, sums_out, copies[-1])


def project_loaded(
    flips, order_hbm, tile_src_hbm, tile_count_hbm, feats, tiles, weights,
    rows_out, sums_out, order, tile_src, tile_count, sems,
):
    copy_all(((order_hbm, order), (tile_src_hbm, tile_src), (tile_count_hbm, tile_count)), sems)
    project_blocks(flips, order, tile_src, tile_count, feats, tiles, weights, rows_out, sums_out)


def first_products(kept_rows, given_rows, own, partner, early, total_out):
    n = own.shape[0]
    total = transposed_product(kept_rows[pl.ds(0, n), :], own[...])
    total += transposed_product(given_rows[pl.ds(0, n), :], partner[...])
    total_out[...] = total + transposed_product(kept_rows[pl.ds(2 * n, early.shape[0]), :], early[...])


def last_products(total, kept_rows, given_rows, late, others_late, others_early, total_out):
    n = late.shape[0]
    last = transposed_product(kept_rows[pl.ds(n, n), :], late[...])
    last += transposed_product(given_rows[pl.ds(2 * n, others_early.shape[0]), :], others_early[...])
    last += transposed_product(given_rows[pl.ds(n, n), :], others_late[...])
    total_out[...] = (total[...] + last).astype(jnp.bfloat16)


def body(n_feat, n_rep, feats, w_self, w_neigh, bias, tile_weight, tile_src, tile_count, owner_order, cotangent):
    block_rows = tile_weight.shape[3]
    tile_slots = tile_weight.shape[2]
    columns = feats.shape[2]
    hidden_units = w_self.shape[1]
    n_chip = n_feat // 2
    rows = n_chip * block_rows

    def swap_cores(value):
        return exchange(value, "feat", n_feat, 1)

    chips = [0, 1] + list(range(n_chip - 1, 1, -1))
    kept_flips = (0,) + tuple(2 * chip + 1 for chip in chips[1:])
    given_flips = tuple(flip ^ 1 for flip in kept_flips)
    tiles_of_slot = jnp.transpose(tile_src, (2, 0, 1))

    operands = (owner_order, tiles_of_slot, tile_count, feats, tile_weight, w_self, w_neigh)
    operands = tuple(pltpu.with_memory_space_constraint(a, pltpu.HBM) for a in operands)
    vmem = pl.BlockSpec(memory_space=pltpu.VMEM)
    params = pltpu.CompilerParams(vmem_limit_bytes=32 * 1024 * 1024)
    hbm = pl.BlockSpec(memory_space=pltpu.HBM)
    indices = [pltpu.SMEM(a.shape, jnp.int32) for a in operands[:3]]

    def results(dtype):
        return (
            jax.ShapeDtypeStruct((rows, 2 * columns), jnp.bfloat16),
            jax.ShapeDtypeStruct((rows, hidden_units), dtype),
        )

    estimate = pl.CostEstimate(
        flops=2 * rows * (tile_slots * block_rows * columns + 2 * columns * hidden_units),
        bytes_accessed=feats.size * 2 + tile_weight.size,
        transcendentals=0,
    )
    given_rows, given, *loaded = pl.pallas_call(
        functools.partial(load_and_project, given_flips),
        out_shape=results(jnp.bfloat16)
        + (
            jax.ShapeDtypeStruct(feats.shape[1:], jnp.bfloat16),
            jax.ShapeDtypeStruct(tile_weight.shape[1:], jnp.bfloat16),
            jax.ShapeDtypeStruct((2 * columns, hidden_units), jnp.bfloat16),
        ),
        in_specs=[hbm] * 7,
        out_specs=(vmem,) * 5,
        scratch_shapes=indices + [pltpu.SemaphoreType.DMA((7,))],
        compiler_params=params,
        cost_estimate=estimate,
    )(*operands)
    kept_rows, kept = pl.pallas_call(
        functools.partial(project_loaded, kept_flips),
        out_shape=results(jnp.float32),
        in_specs=[hbm] * 3 + [vmem] * 3,
        out_specs=(vmem,) * 2,
        scratch_shapes=indices + [pltpu.SemaphoreType.DMA((3,))],
        compiler_params=params,
        cost_estimate=estimate,
    )(*operands[:3], *loaded)

    from_core = swap_cores(given)
    chip_sums = kept + from_core.astype(jnp.float32)
    arrived = [
        exchange(chip_sums[j * block_rows : (j + 1) * block_rows].astype(jnp.bfloat16), "feat", n_feat, kept_flips[j])
        for j in sorted(range(1, n_chip), key=lambda j: (chips[j].bit_count(), -chips[j]))
    ]
    preact = chip_sums[:block_rows] + bias
    for got in arrived:
        preact = preact + got.astype(jnp.float32)
    squash = jax.nn.sigmoid(preact)
    output_grad = (
        cotangent[0].astype(jnp.float32) * squash * (1.0 + preact * (1.0 - squash))
    ).astype(jnp.bfloat16)
    preact, output_grad = lax.optimization_barrier((preact, output_grad))
    hidden = jax.nn.silu(preact).astype(jnp.bfloat16)

    received = [exchange(output_grad, "feat", n_feat, kept_flips[j]) for j in range(1, n_chip)]
    partner = swap_cores(output_grad)
    early = jnp.concatenate(received[1:], axis=0)
    early, partner = lax.optimization_barrier((early, partner))
    others_early = swap_cores(early)
    others_late = swap_cores(received[0])
    products = pl.CostEstimate(flops=2 * rows * 2 * columns * hidden_units, bytes_accessed=0, transcendentals=0)
    total = pl.pallas_call(
        first_products,
        out_shape=jax.ShapeDtypeStruct((2 * columns, hidden_units), jnp.float32),
        in_specs=(vmem,) * 5,
        out_specs=vmem,
        compiler_params=params,
        cost_estimate=products,
    )(kept_rows, given_rows, output_grad, partner, early)
    grads = pl.pallas_call(
        last_products,
        out_shape=jax.ShapeDtypeStruct((2 * columns, hidden_units), jnp.bfloat16),
        in_specs=(vmem,) * 6,
        out_specs=vmem,
        compiler_params=params,
        cost_estimate=products,
    )(total, kept_rows, given_rows, received[0], others_late, others_early)

    n_flips = n_rep.bit_length() - 1
    for step in range(n_flips):
        flips = (2 ** (n_flips - 1 - step), 2 ** (step + 1) - 1)
        sent = lax.optimization_barrier(grads.astype(jnp.bfloat16))
        pairs = [(f * n_rep + r, f * n_rep + (r ^ flips[f % 2])) for f in range(n_feat) for r in range(n_rep)]
        got = lax.ppermute(sent, ("feat", "rep"), pairs)
        grads = sent.astype(jnp.float32) + got.astype(jnp.float32)
    return (hidden[None], grads[:columns], grads[columns:])


def solution(mesh):
    n_feat, n_rep = mesh.shape["feat"], mesh.shape["rep"]

    def local(*args):
        return body(n_feat, n_rep, *args)

    in_specs = (
        P("rep", None, "feat"),
        P("feat", None),
        P("feat", None),
        P(),
        P("rep", None, None, None, None),
        P("rep", None, None),
        P("rep", None),
        P("rep", None),
        P("rep", "feat", None),
    )
    out_specs = (P("rep", "feat", None), P("feat", None), P("feat", None))
    return jax.shard_map(local, mesh=mesh, in_specs=in_specs, out_specs=out_specs, check_vma=False)
```
